32 devices in a mesh: band: 8 (over z, y), grid: 4 (over x, core).
Axes of the slice: x: 2, y: 2, z: 4, core: 2. Of those that a mesh axis runs over, the one named last changes fastest.
Arguments:
- orbitals: float32 [2, 16, 96, 9216], P(None, 'band', 'grid'), may hold values from -7 to 7
- local_potential: float32 [96, 9216], P('grid'), may hold values from 0.5 to 2
- plan: int32 [2], replicated, may hold values from 0 to 7, as said below
- occupancy: int32 [8], replicated, may hold values from 1 to 2, as said below
Outputs:
- new_orbitals: float32 [2, 16, 96, 9216], P(None, 'band', 'grid')
- energies: float32 [16], P('band')
The draws below stay inside these ranges and needn't reach their ends.
Inputs may be any that keep to these rules, and one draw needn't show every extreme that they name: `plan`: distinct band groups, the last group among them. `occupancy`: some group has all 2 orbitals occupied and some group only one.
All inputs are finite; a program needn't handle non-finite values.
Results may differ from the reference program's by a relative error of at most 0.00016.
Values sent between devices are 32-bit elements; how exact they have to be, the bound alone decides.
A program may use at most 128 MiB of HBM per device.

```python
import math
import jax
import jax.numpy as jnp
from jax import lax

G = 96
OB_DEV = 2
ROUNDS = 2
GROUPS = 8
NORB = 16


def draw_orbitals(key, part):
    base = jax.random.fold_in(key, 37)
    first, second_slope, third = jax.random.split(base, 3)
    along_x = jax.random.randint(first, (NORB,), 0, G).astype(jnp.int32)
    across = jax.random.randint(second_slope, (NORB, 2), 0, max(G // 4, 2)).astype(jnp.int32)
    index = jnp.arange(G, dtype=jnp.int32)
    phase_x = along_x[:, None] * index[None, :] % G
    phase_yz = (across[:, 0][:, None, None] * index[None, :, None] + across[:, 1][:, None, None] * index[None, None, :]) % G
    phase_yz = phase_yz.reshape(NORB, G * G)
    total = (phase_x[:, :, None] + phase_yz[:, None, :]) % G
    rotation_argument = total.astype(jnp.float32) * jnp.float32(2.0 * math.pi / G)
    oscillating_drive = jnp.stack([jnp.cos(rotation_argument), jnp.sin(rotation_argument)])
    approximate_guess = jax.random.normal(third, (2, NORB, G, G * G), jnp.float32)
    drive_strength = 3.0
    return jnp.clip(drive_strength * oscillating_drive + approximate_guess, -7.0, 7.0).astype(jnp.float32)


def draw_plan(key, part):
    order = jax.random.permutation(jax.random.fold_in(key, 11), GROUPS).astype(jnp.int32)
    chosen = order[:ROUNDS]
    present = jnp.any(chosen == GROUPS - 1)
    external_driven = chosen.at[ROUNDS - 1].set(GROUPS - 1)
    return jnp.where(present, chosen, external_driven).astype(jnp.int32)


def draw_occupancy(key, part):
    first, second_slope, third = jax.random.split(jax.random.fold_in(key, 23), 3)
    counts = jax.random.randint(first, (GROUPS,), 1, OB_DEV + 1).astype(jnp.int32)
    full_group = jax.random.randint(second_slope, (), 0, GROUPS)
    low_group = (full_group + 1 + jax.random.randint(third, (), 0, GROUPS - 1)) % GROUPS
    counts = counts.at[full_group].set(OB_DEV)
    counts = counts.at[low_group].set(1)
    return counts.astype(jnp.int32)


def levels(stream_key, shape, cuts, least, largest):
    def one(position, blocks):
        heights = jax.random.uniform(jax.random.fold_in(jax.random.fold_in(stream_key, 6), position), (blocks,), jnp.float32, least / len(cuts), largest / len(cuts))
        return jnp.repeat(jnp.exp(heights), shape[position] // blocks).reshape((-1,) + (1,) * (len(shape) - position - 1))

    loudness = one(*cuts[0])
    for cut in cuts[1:]:
        loudness = loudness * one(*cut)
    return loudness


def setup_inputs(seed: int = 0) -> dict:
    splits = jax.random.split(jax.random.key(seed), 5)
    orbitals = draw_orbitals(jax.random.fold_in(splits[4], 71), 0)
    local_potential = jnp.clip(0.5 + 1.5 * jax.random.uniform(splits[1], (G, G * G), jnp.float32) ** levels(splits[1], (G, G * G), ((0, 4),), -0.2, 0.2), 0.5, 2.0)
    plan = draw_plan(jax.random.fold_in(splits[4], 71), 0)
    occupancy = draw_occupancy(jax.random.fold_in(splits[4], 71), 0)
    return {"orbitals": orbitals, "local_potential": local_potential, "plan": plan, "occupancy": occupancy}


TIME_STEP = 0.4
MIXING = 0.25
OMEGA = 0.106
BOX = 65.1


def screened_kernel(freq_x, freq_y, freq_z):
    def fold(index):
        return jnp.where(index <= G // 2, index, index - G).astype(jnp.float32)
    step = 2.0 * math.pi / BOX
    reduce_first_axis = fold(freq_x)[:, None, None]
    fold_y = fold(freq_y)[None, :, None]
    folded_along_z = fold(freq_z)[None, None, :]
    wave = (step * step) * (reduce_first_axis * reduce_first_axis + fold_y * fold_y + folded_along_z * folded_along_z)
    safe = jnp.where(wave > 0, wave, jnp.float32(1.0))
    screen = -jnp.expm1(-wave / (4.0 * OMEGA * OMEGA)) / safe
    return jnp.where(wave > 0, screen, jnp.float32(1.0 / (4.0 * OMEGA * OMEGA)))


def reference(orbitals, local_potential, plan, occupancy):
    psi = orbitals.reshape(2, NORB, G, G, G)
    field = local_potential.reshape(G, G, G)
    k_first = jnp.stack([field * psi[1], -field * psi[0]])
    section = psi + TIME_STEP * k_first
    axis_index = jnp.arange(G, dtype=jnp.int32)
    kernel = screened_kernel(axis_index, axis_index, axis_index)
    exchange = jnp.zeros_like(section)
    for turn in range(ROUNDS):
        source = plan[turn]
        phi = lax.dynamic_slice_in_dim(section, (source * OB_DEV).astype(jnp.int32), OB_DEV, 1)
        count = occupancy[source]
        weight = jnp.where(jnp.arange(OB_DEV, dtype=jnp.int32) < count, 2.0, 0.0).astype(section.dtype)

        def single(orbital):
            dens_re = phi[0] * orbital[0] + phi[1] * orbital[1]
            dens_im = phi[0] * orbital[1] - phi[1] * orbital[0]
            spectrum = jnp.fft.fftn(dens_re + 1j * dens_im, axes=(1, 2, 3))
            pair = jnp.fft.ifftn(kernel * spectrum, axes=(1, 2, 3))
            pot_re = jnp.real(pair).astype(section.dtype)
            imaginary_potential_part = jnp.imag(pair).astype(section.dtype)
            wide = weight[:, None, None, None]
            term_re = jnp.sum(wide * (phi[0] * pot_re - phi[1] * imaginary_potential_part), axis=0)
            term_im = jnp.sum(wide * (phi[0] * imaginary_potential_part + phi[1] * pot_re), axis=0)
            return -MIXING * jnp.stack([term_re, term_im])

        terms = lax.map(single, jnp.moveaxis(section, 1, 0))
        exchange = exchange + jnp.moveaxis(terms, 0, 1)
    hamil = field * section + exchange
    k_second = jnp.stack([hamil[1], -hamil[0]])
    delta = 0.5 * TIME_STEP * (k_first + k_second)
    along = jnp.sum(psi * delta, axis=(0, 2, 3, 4))
    squared_modulus = jnp.sum(delta * delta, axis=(0, 2, 3, 4))
    energy = jnp.sum(section * hamil, axis=(0, 2, 3, 4))
    factor = -2.0 * along / (squared_modulus + 1e-6)
    fresh = psi + factor[None, :, None, None, None] * delta
    orbital_index = jnp.arange(NORB, dtype=jnp.int32)
    filled = jnp.repeat(occupancy, OB_DEV)
    filling = jnp.where(orbital_index % OB_DEV < filled, 2.0, 0.0).astype(section.dtype)
    return fresh.reshape(2, NORB, G, G * G), filling * energy / (G * G * G)
```

```python
import functools
import math

import jax
import jax.numpy as jnp
from jax import lax
from jax.experimental import pallas as pl
from jax.experimental.pallas import tpu as pltpu
from jax.sharding import PartitionSpec as P

MESH = pl.DeviceIdType.MESH
VMEM_BYTES = 56 * 1024 * 1024

TIME_STEP = 0.4
MIXING = 0.25
OMEGA = 0.106
BOX = 65.1


def screened_kernel(points, start, width):
    def square(index):
        fold = jnp.where(index <= points // 2, index, index - points).astype(jnp.float32)
        return fold * fold

    every = square(jnp.arange(points, dtype=jnp.int32))
    part = square(start + jnp.arange(width, dtype=jnp.int32))
    step = 2.0 * math.pi / BOX
    wave = step * step * (every[:, None, None] + part[None, :, None] + every[None, None, :])
    safe = jnp.where(wave > 0, wave, jnp.float32(1.0))
    screen = -jnp.expm1(-wave / (4.0 * OMEGA * OMEGA)) / safe
    return jnp.where(wave > 0, screen, jnp.float32(1.0 / (4.0 * OMEGA * OMEGA)))


def hartley_rows(rows, points):
    product = rows[:, None] * jnp.arange(points, dtype=jnp.int32)[None, :] % points
    angle = product.astype(jnp.float32) * (2.0 * math.pi / points)
    return jnp.cos(angle) + jnp.sin(angle)


def mult(form, left, right):
    return jnp.einsum(form, left, right, precision=lax.Precision.HIGH)


def ring_place(band, bands):
    half = lax.div(band, 2)
    odd = lax.rem(band, 2)
    return (1 - odd) * half + odd * (bands - 1 - half)


def gather_kernel(
    bands,
    plan,
    section,
    cross_out,
    side_out,
    side_cross_out,
    stream_out,
    side_stream_out,
    cross,
    landed,
    stream,
    cross_send,
    cross_recv,
    ring_send,
    ring_recv,
    side_send,
    side_recv,
    keep,
):
    chunks, width = cross.shape[0], cross.shape[-1]
    half = chunks // 2
    steps = landed.shape[1]
    band, here = lax.axis_index("band"), lax.axis_index("grid")
    place = ring_place(band, bands)

    def member(spot):
        back = lax.div(spot, bands // 2)
        return (1 - back) * 2 * spot + back * (2 * (bands - 1 - spot) + 1)

    ring = (
        {"band": member(lax.rem(place + 1, bands))},
        {"band": member(lax.rem(place + bands - 1, bands))},
    )
    partner = {"grid": lax.rem(here + 2, 4)}
    sibling = {"grid": here + 1 - 2 * lax.rem(here, 2)}

    barrier = pltpu.get_barrier_semaphore()
    for other in (*ring, partner, sibling):
        pl.semaphore_signal(barrier, inc=1, device_id=other, device_id_type=MESH)
    pl.semaphore_wait(barrier, 4)

    def remote(source, target, send, recv, device):
        return pltpu.make_async_remote_copy(
            src_ref=source,
            dst_ref=target,
            send_sem=send,
            recv_sem=recv,
            device_id=device,
            device_id_type=MESH,
        )

    def lanes(k):
        return pl.ds(pl.multiple_of(k * width, 128), width)

    def cross_copy(k):
        return remote(
            section.at[:, :, :, lanes(k)], cross.at[k], cross_send.at[k], cross_recv.at[k], partner
        )

    def ring_copy(way, t):
        return remote(
            stream.at[way, t],
            landed.at[way, t],
            ring_send.at[way, t],
            ring_recv.at[way, t],
            ring[way],
        )

    bounds = ((0, half), (half, half), (chunks, steps + 1 - chunks))

    def side_copy(k):
        if k == 0:
            source, target = section, side_out
        elif k == 1:
            source, target = cross, side_cross_out
        else:
            cut = pl.ds(*bounds[k - 2])
            source, target = stream.at[:, cut], side_stream_out.at[:, cut]
        return remote(source, target, side_send.at[k], side_recv.at[k], sibling)

    def keep_copy(k):
        if k == 0:
            return pltpu.make_async_copy(cross, cross_out, keep.at[k])
        cut = pl.ds(*bounds[k - 1])
        return pltpu.make_async_copy(stream.at[:, cut], stream_out.at[:, cut], keep.at[k])

    def store(part):
        side_copy(part + 2).start()
        keep_copy(part + 1).start()

    root = plan[lax.div(here, 2)]
    mine = jnp.full(stream.shape[2:], root, jnp.int32) == band

    @pl.loop(0, half)
    def _(k):
        cross_copy(k).start()
        cross_copy(half + k).start()

    for way in range(2):
        stream[way, 0] = section[:, :, :, way * half * width : (way * half + 1) * width]
        ring_copy(way, 0).start()
    side_copy(0).start()

    @pl.loop(1, half)
    def _(t):
        for way in range(2):
            ring_copy(way, t - 1).wait_recv()
            own = section[:, :, :, lanes(way * half + t)]
            stream[way, t] = jnp.where(mine, own, landed[way, t - 1])
            ring_copy(way, t).start()

    store(0)

    @pl.loop(half, chunks)
    def _(t):
        for way in range(2):
            k = way * half + t - half
            cross_copy(k).wait_recv()
            ring_copy(way, t - 1).wait_recv()
            stream[way, t] = jnp.where(mine, cross[k], landed[way, t - 1])
            ring_copy(way, t).start()

    store(1)
    side_copy(1).start()
    keep_copy(0).start()

    @pl.loop(chunks, steps)
    def _(t):
        for way in range(2):
            ring_copy(way, t - 1).wait_recv()
            stream[way, t] = landed[way, t - 1]
            ring_copy(way, t).start()

    for way in range(2):
        ring_copy(way, steps - 1).wait_recv()
        stream[way, steps] = landed[way, steps - 1]
    store(2)

    @pl.loop(0, chunks)
    def _(k):
        cross_copy(k).wait_send()

    @pl.loop(0, steps)
    def _(t):
        for way in range(2):
            ring_copy(way, t).wait_send()

    for k in range(5):
        side_copy(k).wait()
    for k in range(4):
        keep_copy(k).wait()


def gather(section, plan, bands, width):
    height, plane = section.shape[2], section.shape[3]
    chunks = plane // width
    steps = chunks + bands - 2
    piece = (2, 2, height, width)
    whole = jax.ShapeDtypeStruct((chunks, *piece), jnp.float32)
    log = jax.ShapeDtypeStruct((2, steps + 1, *piece), jnp.float32)
    dma = pltpu.SemaphoreType.DMA
    return pl.pallas_call(
        functools.partial(gather_kernel, bands),
        out_shape=(whole, jax.ShapeDtypeStruct(section.shape, jnp.float32), whole, log, log),
        in_specs=[
            pl.BlockSpec(memory_space=pltpu.SMEM),
            pl.BlockSpec(memory_space=pltpu.VMEM),
        ],
        out_specs=[pl.BlockSpec(memory_space=pl.ANY)] * 5,
        scratch_shapes=[
            pltpu.VMEM(whole.shape, jnp.float32),
            pltpu.VMEM((2, steps, *piece), jnp.float32),
            pltpu.VMEM(log.shape, jnp.float32),
            dma((chunks,)),
            dma((chunks,)),
            dma((2, steps)),
            dma((2, steps)),
            dma((5,)),
            dma((5,)),
            dma((4,)),
        ],
        compiler_params=pltpu.CompilerParams(
            collective_id=0, has_side_effects=True, vmem_limit_bytes=VMEM_BYTES
        ),
    )(plan, section)


def halves(value):
    high = value.astype(jnp.bfloat16)
    return high, (value - high.astype(jnp.float32)).astype(jnp.bfloat16)


def dot(left, right, axis=0):
    return lax.dot_general(
        left, right, (((1,), (axis,)), ((), ())), preferred_element_type=jnp.float32
    )


def three(left, right, axis=0):
    return dot(left[0], right[0], axis) + (dot(left[0], right[1], axis) + dot(left[1], right[0], axis))


def solve_kernel(
    points,
    info,
    weight,
    square_z,
    decay_z,
    s0,
    s1,
    s2,
    s3,
    o0,
    o1,
    o2,
    o3,
    zcut_high,
    zcut_low,
    z_high,
    z_low,
    x_high,
    x_low,
    y_pair,
    y_low,
    square_xy,
    decay_xy,
    near,
    far,
    work,
):
    phase, step = pl.program_id(0), pl.program_id(1)
    width = near.shape[-1]
    tiles = work.shape[0]
    window = zcut_high.shape[2]
    rows = pl.ds(pl.multiple_of(step * width, width), width)

    def source(part, j):
        return jnp.concatenate([s[0, 0, part, j] for s in (s0, s1, s2, s3)], axis=0)

    @pl.when(phase == 0)
    def _():
        own_re, own_im = (
            jnp.concatenate([o0[p, 0], o1[p, 0], o2[0, p, 0], o3[0, p, 0]], axis=0)
            for p in range(2)
        )
        fields = []
        for j in range(2):
            s_re, s_im = source(0, j), source(1, j)
            fields.append(s_re * own_re + s_im * own_im)
            fields.append(s_re * own_im - s_im * own_re)
        high, low = halves(jnp.concatenate(fields, axis=0))
        parts = []
        for k in range(2):
            cut = slice(k * (width - window), k * (width - window) + window)
            parts.append(
                three((zcut_high[k], zcut_low[k]), (high[:, cut], low[:, cut]), 1)
            )
        along = halves(jnp.concatenate(parts, axis=0))
        out = three(along, (x_high[...], x_low[...]))
        for k in range(tiles):
            work[k, rows, :] = out[:, 128 * k : 128 * (k + 1)]

    @pl.when(jnp.logical_and(phase == 0, step == pl.num_programs(1) - 1))
    def _():
        scale = 1.0 / (points * points * points)

        def across(value):
            high, low = halves(value)
            return dot(y_pair[...], jnp.concatenate([high, low], axis=0)) + dot(y_low[...], high)

        @pl.loop(0, points // 4)
        def _(group):
            for pair in range(2):
                first = group * 4 + pair * 2
                lines = [pl.ds(first + u, points, stride=points) for u in range(2)]
                value = jnp.concatenate(
                    [work[k, line, :] for line in lines for k in range(tiles)], axis=1
                )
                factors = []
                for u in range(2):
                    wave = square_xy[...] + square_z[first + u]
                    safe = jnp.where(wave > 0, wave, 1.0)
                    screen = (scale - decay_xy[...] * (decay_z[first + u] * scale)) / safe
                    factors.append(
                        jnp.where(wave > 0, screen, scale / (4.0 * OMEGA * OMEGA))
                    )
                value = across(across(value) * jnp.concatenate(factors, axis=1))
                for u in range(2):
                    for k in range(tiles):
                        at = 128 * (u * tiles + k)
                        work[k, lines[u], :] = value[:, at : at + 128]

    @pl.when(phase == 1)
    def _():
        spectrum = halves(jnp.concatenate([work[k, rows, :] for k in range(tiles)], axis=1))
        along = halves(three((x_high[...], x_low[...]), spectrum, 1))
        field = three(along, (z_high[...], z_low[...]))
        term_re = term_im = 0.0
        for j in range(2):
            v_re = field[2 * j * points : (2 * j + 1) * points]
            v_im = field[(2 * j + 1) * points : (2 * j + 2) * points]
            s_re, s_im = source(0, j), source(1, j)
            term_re = term_re + weight[j] * (s_re * v_re - s_im * v_im)
            term_im = term_im + weight[j] * (s_re * v_im + s_im * v_re)
        middle = points // 2
        for k, term in enumerate((term_re, term_im)):
            near[k] = term[:middle]
            far[k] = term[middle:]


def solve(section, gathered, plan, weights, along_x, bands, width):
    cross, side, side_cross, stream, side_stream = gathered
    height, plane = section.shape[2], section.shape[3]
    points = along_x.shape[0]
    chunks = plane // width
    half = chunks // 2
    here = lax.axis_index("grid")
    place = ring_place(lax.axis_index("band"), bands)
    root = ring_place(jnp.where(here // 2 == 0, plan[0], plan[1]), bands)
    info = jnp.stack(
        [lax.rem(place - root + bands, bands), lax.rem(root - place + bands, bands), here % 2]
    ).astype(jnp.int32)

    index = jnp.arange(points, dtype=jnp.int32)
    along = hartley_rows(index, points)
    four = jnp.eye(4, dtype=jnp.float32)

    def blocks(matrix):
        return jnp.einsum("ab,ij->aibj", four, matrix).reshape(width, width)

    def split(value):
        high = lax.reduce_precision(value, 8, 7)
        return high.astype(jnp.bfloat16), (value - high).astype(jnp.bfloat16)

    z_high, z_low = split(blocks(along))
    x_high, x_low = split(blocks(along_x))
    y_high, y_low = split(along)
    window = -(-(width // 2) // 128) * 128

    def cuts(matrix):
        return jnp.stack([matrix[: width // 2, :window], matrix[width // 2 :, width - window :]])

    fold = jnp.where(index <= points // 2, index, index - points).astype(jnp.float32)
    base = 2.0 * math.pi / BOX
    square = base * base * (fold * fold)
    decay = jnp.exp(-square / (4.0 * OMEGA * OMEGA))
    square_x, decay_x = jnp.tile(square, 4), jnp.tile(decay, 4)
    square_xy = square[:, None] + square_x[None, :]
    decay_xy = decay[:, None] * decay_x[None, :]
    tables = [
        cuts(z_high),
        cuts(z_low),
        z_high,
        z_low,
        x_high,
        x_low,
        jnp.concatenate([y_high, y_high], axis=1),
        y_low,
        square_xy,
        decay_xy,
    ]

    def line(offset):
        def spot(p, i, info):
            way = lax.div(i, half)
            return (way, info[way] + lax.rem(i, half) + offset, 0, 0, 0, 0)

        return pl.BlockSpec((1, 1, 2, 2, height, width), spot)

    natural = pl.BlockSpec(
        (2, 1, height, width), lambda p, i, info: (0, info[2], 0, (1 - p) * i + p * (chunks - 1))
    )
    piece = pl.BlockSpec(
        (1, 2, 1, height, width),
        lambda p, i, info: ((1 - p) * i + p * (chunks - 1), 0, info[2], 0, 0),
    )
    scalars = pl.BlockSpec(memory_space=pltpu.SMEM)
    result = pl.BlockSpec((2, 2 * height, width), lambda p, i, info: (0, 0, p * i))

    def full(table):
        return pl.BlockSpec(table.shape, lambda p, i, info: (0,) * table.ndim)

    half_grid = jax.ShapeDtypeStruct((2, 2 * height, plane), jnp.float32)
    return pl.pallas_call(
        functools.partial(solve_kernel, points),
        grid_spec=pltpu.PrefetchScalarGridSpec(
            num_scalar_prefetch=1,
            grid=(2, chunks),
            in_specs=[scalars] * 3
            + [line(0), line(0), line(half), line(half)]
            + [natural, natural, piece, piece]
            + [full(table) for table in tables],
            out_specs=[result, result],
            scratch_shapes=[pltpu.VMEM((width // 128, plane, 128), jnp.float32)],
        ),
        out_shape=(half_grid, half_grid),
        compiler_params=pltpu.CompilerParams(
            dimension_semantics=("arbitrary", "arbitrary"), vmem_limit_bytes=VMEM_BYTES
        ),
    )(
        info,
        weights,
        square,
        decay,
        stream,
        side_stream,
        stream,
        side_stream,
        section,
        side,
        cross,
        side_cross,
        *tables,
    )


def per_device(orbitals, local_potential, plan, occupancy):
    rounds = plan.shape[0]
    count_own = orbitals.shape[1]
    height = orbitals.shape[2]
    plane = orbitals.shape[3]
    points = math.isqrt(plane)
    devices = lax.axis_size("grid")
    parts = devices // 4
    here = lax.axis_index("grid")
    share, slot = here // parts, here % parts
    first_core, first_chip = share % 2 == 0, share // 2 == 0
    teams = [[q * parts + s for s in range(parts)] for q in range(4)]

    def swap(value, bit):
        return lax.ppermute(
            value, "grid", [(g, ((g // parts) ^ bit) * parts + g % parts) for g in range(devices)]
        )

    def core_swap(value):
        return swap(value, 1)

    def chip_swap(value):
        return swap(value, 2)

    def turn(value, split, concat):
        if parts == 1:
            return value
        return lax.all_to_all(
            value, "grid", split, concat, axis_index_groups=teams, tiled=True
        )

    k_first = jnp.stack([local_potential * orbitals[1], -local_potential * orbitals[0]])
    section = orbitals + TIME_STEP * k_first

    band = lax.axis_index("band")

    def spread(orbital):
        return lax.psum(
            jnp.stack([jnp.where(band == plan[r], orbital, 0.0) for r in range(rounds)]), "band"
        )

    def collect(both):
        near = jnp.where(first_chip, both[0], both[1])
        far = chip_swap(jnp.where(first_chip, both[1], both[0]))
        pair = jnp.stack([near, far])
        other = core_swap(pair)
        return jnp.concatenate([near, other[0], far, other[1]], axis=1)

    block = jnp.arange(parts)[:, None] + jnp.stack([(share ^ k) * parts for k in range(4)])
    order = block[:, :, None] * height + jnp.arange(height, dtype=jnp.int32)
    along_x = hartley_rows(order.reshape(points), points)
    ways = along_x.reshape(parts, 4, height, points)
    width = points // parts
    along = hartley_rows(jnp.arange(points, dtype=jnp.int32), points)
    source_group = jnp.where(first_chip, plan[0], plan[1])
    groups = jnp.arange(occupancy.shape[0], dtype=jnp.int32)
    filled = jnp.sum(jnp.where(groups == source_group, occupancy, 0))

    weights = [jnp.where(j < filled, 2.0, 0.0).astype(jnp.float32) for j in range(count_own)]
    bands = lax.axis_size("band")
    span = 4 * points
    if parts == 1 and span % 128 == 0 and height % 8 == 0 and count_own == rounds == 2 and bands > 2:
        scaled = -MIXING * jnp.stack(weights)
        gathered = gather(section, plan, bands, span)
        near, far = solve(section, gathered, plan, scaled, along_x, bands, span)
        far = chip_swap(far)
    else:
        mine = jnp.where(first_core, section[:, 0], section[:, 1])
        give = jnp.where(first_core, section[:, 1], section[:, 0])
        half = jnp.concatenate([mine, core_swap(give)], axis=1)
        own = jnp.concatenate([half, chip_swap(half)], axis=1)

        kernel = screened_kernel(points, slot * width, width) * (1.0 / (points * points * points))
        def spectrum(source):
            dens_re = source[0] * own[0] + source[1] * own[1]
            dens_im = source[0] * own[1] - source[1] * own[0]
            field = jnp.stack([dens_re, dens_im]).reshape(2, 4 * height, points, points)
            field = mult("pxyz,zk->pxyk", field, along)
            field = turn(mult("pxyz,yk->pxkz", field, along), 2, 1)
            return mult("pxyz,xk->pkyz", field, along_x) * kernel

        def potential_term(source, weight, moved, side):
            rows = ways[:, 2 * side : 2 * side + 2].reshape(-1, points)
            field = turn(mult("pxyz,kx->pkyz", moved, rows), 1, 2)
            field = mult("pxyz,yk->pxkz", field, along)
            field = mult("pxyz,zk->pxyk", field, along)
            v_re, v_im = field.reshape(2, 2 * height, plane)
            s_re, s_im = source[:, 2 * side * height : 2 * (side + 1) * height]
            scale = -MIXING * weight
            return jnp.stack([scale * (s_re * v_re - s_im * v_im), scale * (s_re * v_im + s_im * v_re)])

        both = [spread(section[:, 0])]
        for j in range(1, count_own):
            both[j - 1], orbital = lax.optimization_barrier((both[j - 1], section[:, j]))
            both.append(spread(orbital))
        near = far = 0.0
        for j in range(count_own):
            if j > 0:
                both[j], near, far = lax.optimization_barrier((both[j], near, far))
            source = collect(both[j])
            moved = spectrum(source)
            far = far + potential_term(source, weights[j], moved, 1)
            if j == count_own - 1:
                far = chip_swap(far)
            near = near + potential_term(source, weights[j], moved, 0)
    total = near + far
    kept = total[:, :height]
    got = core_swap(total[:, height:])
    exchange = jnp.stack(
        [jnp.where(first_core, kept, got), jnp.where(first_core, got, kept)], axis=1
    )

    hamil = local_potential * section + exchange
    k_second = jnp.stack([hamil[1], -hamil[0]])
    delta = 0.5 * TIME_STEP * (k_first + k_second)
    inner = jnp.sum(orbitals * delta, axis=(0, 2, 3))
    squared_modulus = jnp.sum(delta * delta, axis=(0, 2, 3))
    energy = jnp.sum(section * hamil, axis=(0, 2, 3))
    inner, squared_modulus, energy = lax.psum(jnp.stack([inner, squared_modulus, energy]), "grid")
    factor = -2.0 * inner / (squared_modulus + 1e-06)
    fresh = orbitals + factor[None, :, None, None] * delta
    own_filled = jnp.sum(jnp.where(groups == band, occupancy, 0))
    filling = jnp.where(jnp.arange(count_own, dtype=jnp.int32) < own_filled, 2.0, 0.0).astype(
        jnp.float32
    )
    return (fresh, filling * energy / (points * points * points))


def solution(mesh):
    return jax.shard_map(
        per_device,
        mesh=mesh,
        in_specs=(P(None, "band", "grid", None), P("grid", None), P(), P()),
        out_specs=(P(None, "band", "grid", None), P("band")),
        check_vma=False,
    )
```

```python
import functools
import math

import jax
import jax.numpy as jnp
import ml_dtypes
import numpy as np
from jax import lax
from jax.experimental import pallas as pl
from jax.experimental.pallas import tpu as pltpu
from jax.sharding import PartitionSpec as P

MESH = pl.DeviceIdType.MESH
VMEM_BYTES = 56 * 1024 * 1024

TIME_STEP = 0.4
MIXING = 0.25
OMEGA = 0.106
BOX = 65.1


def screened_kernel(points, start, width):
    def square(index):
        fold = jnp.where(index <= points // 2, index, index - points).astype(jnp.float32)
        return fold * fold

    every = square(jnp.arange(points, dtype=jnp.int32))
    part = square(start + jnp.arange(width, dtype=jnp.int32))
    step = 2.0 * math.pi / BOX
    wave = step * step * (every[:, None, None] + part[None, :, None] + every[None, None, :])
    safe = jnp.where(wave > 0, wave, jnp.float32(1.0))
    screen = -jnp.expm1(-wave / (4.0 * OMEGA * OMEGA)) / safe
    return jnp.where(wave > 0, screen, jnp.float32(1.0 / (4.0 * OMEGA * OMEGA)))


def hartley_rows(rows, points):
    product = rows[:, None] * jnp.arange(points, dtype=jnp.int32)[None, :] % points
    angle = product.astype(jnp.float32) * (2.0 * math.pi / points)
    return jnp.cos(angle) + jnp.sin(angle)


def mult(form, left, right):
    return jnp.einsum(form, left, right, precision=lax.Precision.HIGH)


def ring_place(band, bands):
    half = lax.div(band, 2)
    odd = lax.rem(band, 2)
    return (1 - odd) * half + odd * (bands - 1 - half)


def gather_kernel(
    bands,
    plan,
    section,
    cross_out,
    side_out,
    side_cross_out,
    stream_out,
    side_stream_out,
    cross,
    landed,
    stream,
    cross_send,
    cross_recv,
    ring_send,
    ring_recv,
    side_send,
    side_recv,
    keep,
):
    chunks, width = cross.shape[0], cross.shape[-1]
    half = chunks // 2
    steps = landed.shape[1]
    band, here = lax.axis_index("band"), lax.axis_index("grid")
    place = ring_place(band, bands)

    def member(spot):
        back = lax.div(spot, bands // 2)
        return (1 - back) * 2 * spot + back * (2 * (bands - 1 - spot) + 1)

    ring = (
        {"band": member(lax.rem(place + 1, bands))},
        {"band": member(lax.rem(place + bands - 1, bands))},
    )
    partner = {"grid": lax.rem(here + 2, 4)}
    sibling = {"grid": here + 1 - 2 * lax.rem(here, 2)}

    barrier = pltpu.get_barrier_semaphore()
    for other in (*ring, partner, sibling):
        pl.semaphore_signal(barrier, inc=1, device_id=other, device_id_type=MESH)
    pl.semaphore_wait(barrier, 4)

    def remote(source, target, send, recv, device):
        return pltpu.make_async_remote_copy(
            src_ref=source,
            dst_ref=target,
            send_sem=send,
            recv_sem=recv,
            device_id=device,
            device_id_type=MESH,
        )

    def lanes(k):
        return pl.ds(pl.multiple_of(k * width, 128), width)

    def cross_copy(k):
        return remote(
            section.at[:, :, :, lanes(k)], cross.at[k], cross_send.at[k], cross_recv.at[k], partner
        )

    lines = [(way, part) for part in range(2) for way in range(2)]

    def ring_copy(way, part, t):
        return remote(
            stream.at[way, t, part],
            landed.at[way, t, part],
            ring_send.at[way, part, t],
            ring_recv.at[way, part, t],
            ring[way],
        )

    bounds = ((0, half), (half, half), (chunks, steps + 1 - chunks))

    def side_copy(k):
        if k == 0:
            source, target = section, side_out
        elif k == 1:
            source, target = cross, side_cross_out
        else:
            cut = pl.ds(*bounds[k - 2])
            source, target = stream.at[:, cut], side_stream_out.at[:, cut]
        return remote(source, target, side_send.at[k], side_recv.at[k], sibling)

    def keep_copy(k):
        if k == 0:
            return pltpu.make_async_copy(cross, cross_out, keep.at[k])
        cut = pl.ds(*bounds[k - 1])
        return pltpu.make_async_copy(stream.at[:, cut], stream_out.at[:, cut], keep.at[k])

    def store(part):
        side_copy(part + 2).start()
        keep_copy(part + 1).start()

    root = plan[lax.div(here, 2)]
    mine = jnp.full(stream.shape[3:], root, jnp.int32) == band

    @pl.loop(0, half)
    def _(k):
        cross_copy(k).start()
        cross_copy(half + k).start()

    for way, part in lines:
        stream[way, 0, part] = section[part, :, :, way * half * width : (way * half + 1) * width]
        ring_copy(way, part, 0).start()
    side_copy(0).start()

    @pl.loop(1, half)
    def _(t):
        for way, part in lines:
            ring_copy(way, part, t - 1).wait_recv()
            own = section[part, :, :, lanes(way * half + t)]
            stream[way, t, part] = jnp.where(mine, own, landed[way, t - 1, part])
            ring_copy(way, part, t).start()

    store(0)

    @pl.loop(half, chunks)
    def _(t):
        for way in range(2):
            cross_copy(way * half + t - half).wait_recv()
        for way, part in lines:
            ring_copy(way, part, t - 1).wait_recv()
            own = cross[way * half + t - half, part]
            stream[way, t, part] = jnp.where(mine, own, landed[way, t - 1, part])
            ring_copy(way, part, t).start()

    store(1)
    side_copy(1).start()
    keep_copy(0).start()

    @pl.loop(chunks, steps)
    def _(t):
        for way, part in lines:
            ring_copy(way, part, t - 1).wait_recv()
            stream[way, t, part] = landed[way, t - 1, part]
            ring_copy(way, part, t).start()

    for way, part in lines:
        ring_copy(way, part, steps - 1).wait_recv()
        stream[way, steps, part] = landed[way, steps - 1, part]
    store(2)

    @pl.loop(0, chunks)
    def _(k):
        cross_copy(k).wait_send()

    @pl.loop(0, steps)
    def _(t):
        for way, part in lines:
            ring_copy(way, part, t).wait_send()

    for k in range(5):
        side_copy(k).wait()
    for k in range(4):
        keep_copy(k).wait()


def gather(section, plan, bands, width):
    height, plane = section.shape[2], section.shape[3]
    chunks = plane // width
    steps = chunks + bands - 2
    piece = (2, 2, height, width)
    whole = jax.ShapeDtypeStruct((chunks, *piece), jnp.float32)
    log = jax.ShapeDtypeStruct((2, steps + 1, *piece), jnp.float32)
    dma = pltpu.SemaphoreType.DMA
    return pl.pallas_call(
        functools.partial(gather_kernel, bands),
        out_shape=(whole, jax.ShapeDtypeStruct(section.shape, jnp.float32), whole, log, log),
        in_specs=[
            pl.BlockSpec(memory_space=pltpu.SMEM),
            pl.BlockSpec(memory_space=pltpu.VMEM),
        ],
        out_specs=[pl.BlockSpec(memory_space=pl.ANY)] * 5,
        scratch_shapes=[
            pltpu.VMEM(whole.shape, jnp.float32),
            pltpu.VMEM((2, steps, *piece), jnp.float32),
            pltpu.VMEM(log.shape, jnp.float32),
            dma((chunks,)),
            dma((chunks,)),
            dma((2, 2, steps)),
            dma((2, 2, steps)),
            dma((5,)),
            dma((5,)),
            dma((4,)),
        ],
        compiler_params=pltpu.CompilerParams(
            collective_id=0, has_side_effects=True, vmem_limit_bytes=VMEM_BYTES
        ),
    )(plan, section)


def halves(value):
    high = value.astype(jnp.bfloat16)
    return high, (value - high.astype(jnp.float32)).astype(jnp.bfloat16)


def dot(left, right, axis=0):
    return lax.dot_general(
        left, right, (((1,), (axis,)), ((), ())), preferred_element_type=jnp.float32
    )


def three(left, right, axis=0):
    return dot(left[0], right[0], axis) + (dot(left[0], right[1], axis) + dot(left[1], right[0], axis))


def concat(pieces):
    return jnp.concatenate(pieces, axis=0)


def forward_kernel(
    points,
    info,
    square_z,
    decay_z,
    s0,
    s1,
    s2,
    s3,
    o0,
    o1,
    o2,
    o3,
    zcut_high,
    zcut_low,
    x_high,
    x_low,
    y_pair,
    y_low,
    square_xy,
    decay_xy,
    work,
):
    step = pl.program_id(0)
    width = x_high.shape[0]
    tiles = work.shape[0]
    window = zcut_high.shape[2]
    rows = pl.ds(pl.multiple_of(step * width, width), width)

    def source(part, j):
        return concat([s[0, 0, part, j] for s in (s0, s1, s2, s3)])

    own_re, own_im = (
        jnp.concatenate([o0[p, 0], o1[p, 0], o2[0, p, 0], o3[0, p, 0]], axis=0)
        for p in range(2)
    )
    fields = []
    for j in range(2):
        s_re, s_im = source(0, j), source(1, j)
        fields.append(s_re * own_re + s_im * own_im)
        fields.append(s_re * own_im - s_im * own_re)
    high, low = halves(jnp.concatenate(fields, axis=0))
    parts = []
    for k in range(2):
        cut = slice(k * (width - window), k * (width - window) + window)
        parts.append(
            three((zcut_high[k], zcut_low[k]), (high[:, cut], low[:, cut]), 1)
        )
    along = halves(jnp.concatenate(parts, axis=0))
    out = three(along, (x_high[...], x_low[...]))
    for k in range(tiles):
        work[k, rows, :] = out[:, 128 * k : 128 * (k + 1)]

    @pl.when(step == pl.num_programs(0) - 1)
    def _():
        scale = 1.0 / (points * points * points)

        def across(value):
            high, low = halves(value)
            return dot(y_pair[...], jnp.concatenate([high, low], axis=0)) + dot(y_low[...], high)

        @pl.loop(0, points // 4)
        def _(group):
            for pair in range(2):
                first = group * 4 + pair * 2
                lines = [pl.ds(first + u, points, stride=points) for u in range(2)]
                value = jnp.concatenate(
                    [work[k, line, :] for line in lines for k in range(tiles)], axis=1
                )
                factors = []
                for u in range(2):
                    wave = square_xy[...] + square_z[first + u]
                    safe = jnp.where(wave > 0, wave, 1.0)
                    screen = (scale - decay_xy[...] * (decay_z[first + u] * scale)) / safe
                    factors.append(
                        jnp.where(wave > 0, screen, scale / (4.0 * OMEGA * OMEGA))
                    )
                value = across(across(value) * jnp.concatenate(factors, axis=1))
                for u in range(2):
                    for k in range(tiles):
                        at = 128 * (u * tiles + k)
                        work[k, lines[u], :] = value[:, at : at + 128]

def inverse_kernel(info, weight, work, s0, s1, x_high, x_low, z_high, z_low, term):
    middle = term.shape[1]
    spectrum = halves(jnp.concatenate([work[k] for k in range(work.shape[0])], axis=1))
    along = halves(three((x_high[...], x_low[...]), spectrum, 1))
    field = three(along, (z_high[...], z_low[...]))
    term_re = term_im = 0.0
    for j in range(2):
        v_re = field[2 * j * middle : (2 * j + 1) * middle]
        v_im = field[(2 * j + 1) * middle : (2 * j + 2) * middle]
        s_re, s_im = (concat([s[0, 0, part, j] for s in (s0, s1)]) for part in range(2))
        term_re = term_re + weight[j] * (s_re * v_re - s_im * v_im)
        term_im = term_im + weight[j] * (s_re * v_im + s_im * v_re)
    term[0] = term_re
    term[1] = term_im


def numpy_hartley(points):
    index = np.arange(points)
    angle = index[:, None] * index[None, :] % points * (2.0 * math.pi / points)
    return np.cos(angle) + np.sin(angle)


def numpy_split(value):
    high = value.astype(ml_dtypes.bfloat16)
    return high, (value - high.astype(np.float64)).astype(ml_dtypes.bfloat16)


def solve(section, gathered, plan, weights, bands, width):
    cross, side, side_cross, stream, side_stream = gathered
    height, plane = section.shape[2], section.shape[3]
    points = 4 * height
    chunks = plane // width
    half = chunks // 2
    middle = points // 2
    here = lax.axis_index("grid")
    place = ring_place(lax.axis_index("band"), bands)
    root = ring_place(jnp.where(here // 2 == 0, plan[0], plan[1]), bands)
    info = jnp.stack(
        [lax.rem(place - root + bands, bands), lax.rem(root - place + bands, bands), here % 2]
    ).astype(jnp.int32)

    along = numpy_hartley(points)
    orders = [
        np.concatenate([(g ^ k) * height + np.arange(height) for k in range(4)]) for g in range(4)
    ]
    x_all = np.stack([np.kron(np.eye(4), along[order]) for order in orders])
    x_sides = x_all.reshape(4, 4, 2, middle, width)

    def pick(table):
        return [
            lax.dynamic_index_in_dim(jnp.asarray(piece), here, 0, keepdims=False)
            for piece in numpy_split(table)
        ]

    x_high, x_low = pick(x_all)
    z_high, z_low = numpy_split(np.kron(np.eye(4), along))
    y_high, y_low = numpy_split(along)
    window = -(-(width // 2) // 128) * 128

    def cuts(matrix):
        return jnp.asarray(
            np.stack([matrix[: width // 2, :window], matrix[width // 2 :, width - window :]])
        )

    index = np.arange(points)
    fold = np.where(index <= points // 2, index, index - points)
    square = (2.0 * math.pi / BOX) ** 2 * (fold * fold)
    decay = np.exp(-square / (4.0 * OMEGA * OMEGA))

    def single(value):
        return jnp.asarray(value.astype(np.float32))

    tables = [
        cuts(z_high),
        cuts(z_low),
        x_high,
        x_low,
        jnp.asarray(np.concatenate([y_high, y_high], axis=1)),
        jnp.asarray(y_low),
        single(square[:, None] + np.tile(square, 4)[None, :]),
        single(decay[:, None] * np.tile(decay, 4)[None, :]),
    ]

    def line(offset):
        def spot(i, info):
            way = lax.div(i, half)
            return (way, info[way] + lax.rem(i, half) + offset, 0, 0, 0, 0)

        return pl.BlockSpec((1, 1, 2, 2, height, width), spot)

    natural = pl.BlockSpec((2, 1, height, width), lambda i, info: (0, info[2], 0, i))
    piece = pl.BlockSpec((1, 2, 1, height, width), lambda i, info: (i, 0, info[2], 0, 0))
    scalars = pl.BlockSpec(memory_space=pltpu.SMEM)
    tiles = width // 128

    def full(table):
        return pl.BlockSpec(table.shape, lambda i, info: (0,) * table.ndim)

    spectrum = jax.ShapeDtypeStruct((tiles, plane, 128), jnp.float32)
    params = pltpu.CompilerParams(
        dimension_semantics=("arbitrary",), vmem_limit_bytes=VMEM_BYTES
    )
    work = pl.pallas_call(
        functools.partial(forward_kernel, points),
        grid_spec=pltpu.PrefetchScalarGridSpec(
            num_scalar_prefetch=1,
            grid=(chunks,),
            in_specs=[scalars] * 2
            + [line(0), line(0), line(half), line(half)]
            + [natural, natural, piece, piece]
            + [full(table) for table in tables],
            out_specs=full(spectrum),
        ),
        out_shape=spectrum,
        compiler_params=params,
    )(
        info,
        single(square),
        single(decay),
        stream,
        side_stream,
        stream,
        side_stream,
        section,
        side,
        cross,
        side_cross,
        *tables,
    )

    def inverse(part):
        constants = [
            *pick(x_sides[:, :, part].reshape(4, 4 * middle, width)),
            jnp.asarray(z_high),
            jnp.asarray(z_low),
        ]
        return pl.pallas_call(
            inverse_kernel,
            grid_spec=pltpu.PrefetchScalarGridSpec(
                num_scalar_prefetch=1,
                grid=(chunks,),
                in_specs=[scalars, pl.BlockSpec((tiles, width, 128), lambda i, info: (0, i, 0))]
                + [line(part * half)] * 2
                + [full(table) for table in constants],
                out_specs=pl.BlockSpec((2, middle, width), lambda i, info: (0, 0, i)),
            ),
            out_shape=jax.ShapeDtypeStruct((2, middle, plane), jnp.float32),
            compiler_params=params,
            cost_estimate=pl.CostEstimate(
                flops=24 * middle * width * plane, bytes_accessed=32 * plane * width, transcendentals=0
            ),
        )(info, weights, work, stream, side_stream, *constants)

    return inverse


def per_device(orbitals, local_potential, plan, occupancy):
    rounds = plan.shape[0]
    count_own = orbitals.shape[1]
    height = orbitals.shape[2]
    plane = orbitals.shape[3]
    points = math.isqrt(plane)
    devices = lax.axis_size("grid")
    parts = devices // 4
    here = lax.axis_index("grid")
    share, slot = here // parts, here % parts
    first_core, first_chip = share % 2 == 0, share // 2 == 0
    teams = [[q * parts + s for s in range(parts)] for q in range(4)]

    def swap(value, bit):
        return lax.ppermute(
            value, "grid", [(g, ((g // parts) ^ bit) * parts + g % parts) for g in range(devices)]
        )

    def core_swap(value):
        return swap(value, 1)

    def chip_swap(value):
        return swap(value, 2)

    def turn(value, split, concat):
        if parts == 1:
            return value
        return lax.all_to_all(
            value, "grid", split, concat, axis_index_groups=teams, tiled=True
        )

    k_first = jnp.stack([local_potential * orbitals[1], -local_potential * orbitals[0]])
    section = orbitals + TIME_STEP * k_first

    band = lax.axis_index("band")

    def spread(orbital):
        return lax.psum(
            jnp.stack([jnp.where(band == plan[r], orbital, 0.0) for r in range(rounds)]), "band"
        )

    def collect(both):
        near = jnp.where(first_chip, both[0], both[1])
        far = chip_swap(jnp.where(first_chip, both[1], both[0]))
        pair = jnp.stack([near, far])
        other = core_swap(pair)
        return jnp.concatenate([near, other[0], far, other[1]], axis=1)

    block = jnp.arange(parts)[:, None] + jnp.stack([(share ^ k) * parts for k in range(4)])
    order = block[:, :, None] * height + jnp.arange(height, dtype=jnp.int32)
    along_x = hartley_rows(order.reshape(points), points)
    ways = along_x.reshape(parts, 4, height, points)
    width = points // parts
    along = hartley_rows(jnp.arange(points, dtype=jnp.int32), points)
    source_group = jnp.where(first_chip, plan[0], plan[1])
    groups = jnp.arange(occupancy.shape[0], dtype=jnp.int32)
    filled = jnp.sum(jnp.where(groups == source_group, occupancy, 0))

    weights = [jnp.where(j < filled, 2.0, 0.0).astype(jnp.float32) for j in range(count_own)]
    bands = lax.axis_size("band")
    span = 4 * points
    if parts == 1 and span % 128 == 0 and height % 8 == 0 and count_own == rounds == 2 and bands > 2:
        scaled = -MIXING * jnp.stack(weights)
        gathered = gather(section, plan, bands, span)
        inverse = solve(section, gathered, plan, scaled, bands, span)
        far = chip_swap(inverse(1))
        near = inverse(0)
    else:
        mine = jnp.where(first_core, section[:, 0], section[:, 1])
        give = jnp.where(first_core, section[:, 1], section[:, 0])
        half = jnp.concatenate([mine, core_swap(give)], axis=1)
        own = jnp.concatenate([half, chip_swap(half)], axis=1)

        kernel = screened_kernel(points, slot * width, width) * (1.0 / (points * points * points))
        def spectrum(source):
            dens_re = source[0] * own[0] + source[1] * own[1]
            dens_im = source[0] * own[1] - source[1] * own[0]
            field = jnp.stack([dens_re, dens_im]).reshape(2, 4 * height, points, points)
            field = mult("pxyz,zk->pxyk", field, along)
            field = turn(mult("pxyz,yk->pxkz", field, along), 2, 1)
            return mult("pxyz,xk->pkyz", field, along_x) * kernel

        def potential_term(source, weight, moved, side):
            rows = ways[:, 2 * side : 2 * side + 2].reshape(-1, points)
            field = turn(mult("pxyz,kx->pkyz", moved, rows), 1, 2)
            field = mult("pxyz,yk->pxkz", field, along)
            field = mult("pxyz,zk->pxyk", field, along)
            v_re, v_im = field.reshape(2, 2 * height, plane)
            s_re, s_im = source[:, 2 * side * height : 2 * (side + 1) * height]
            scale = -MIXING * weight
            return jnp.stack([scale * (s_re * v_re - s_im * v_im), scale * (s_re * v_im + s_im * v_re)])

        both = [spread(section[:, 0])]
        for j in range(1, count_own):
            both[j - 1], orbital = lax.optimization_barrier((both[j - 1], section[:, j]))
            both.append(spread(orbital))
        near = far = 0.0
        for j in range(count_own):
            if j > 0:
                both[j], near, far = lax.optimization_barrier((both[j], near, far))
            source = collect(both[j])
            moved = spectrum(source)
            far = far + potential_term(source, weights[j], moved, 1)
            if j == count_own - 1:
                far = chip_swap(far)
            near = near + potential_term(source, weights[j], moved, 0)
    got = core_swap(near[:, height:] + far[:, height:])
    kept = near[:, :height] + far[:, :height]
    exchange = jnp.stack(
        [jnp.where(first_core, kept, got), jnp.where(first_core, got, kept)], axis=1
    )

    hamil = local_potential * section + exchange
    k_second = jnp.stack([hamil[1], -hamil[0]])
    delta = 0.5 * TIME_STEP * (k_first + k_second)
    inner = jnp.sum(orbitals * delta, axis=(0, 2, 3))
    squared_modulus = jnp.sum(delta * delta, axis=(0, 2, 3))
    energy = jnp.sum(section * hamil, axis=(0, 2, 3))
    inner, squared_modulus, energy = lax.psum(jnp.stack([inner, squared_modulus, energy]), "grid")
    factor = -2.0 * inner / (squared_modulus + 1e-06)
    fresh = orbitals + factor[None, :, None, None] * delta
    own_filled = jnp.sum(jnp.where(groups == band, occupancy, 0))
    filling = jnp.where(jnp.arange(count_own, dtype=jnp.int32) < own_filled, 2.0, 0.0).astype(
        jnp.float32
    )
    return (fresh, filling * energy / (points * points * points))


def solution(mesh):
    return jax.shard_map(
        per_device,
        mesh=mesh,
        in_specs=(P(None, "band", "grid", None), P("grid", None), P(), P()),
        out_specs=(P(None, "band", "grid", None), P("band")),
        check_vma=False,
    )
```

```python
import functools
import math

import jax
import jax.numpy as jnp
import ml_dtypes
import numpy as np
from jax import lax
from jax.experimental import pallas as pl
from jax.experimental.pallas import tpu as pltpu
from jax.sharding import PartitionSpec as P

MESH = pl.DeviceIdType.MESH
VMEM_BYTES = 56 * 1024 * 1024

TIME_STEP = 0.4
MIXING = 0.25
OMEGA = 0.106
BOX = 65.1


def screened_kernel(points, start, width):
    def square(index):
        fold = jnp.where(index <= points // 2, index, index - points).astype(jnp.float32)
        return fold * fold

    every = square(jnp.arange(points, dtype=jnp.int32))
    part = square(start + jnp.arange(width, dtype=jnp.int32))
    step = 2.0 * math.pi / BOX
    wave = step * step * (every[:, None, None] + part[None, :, None] + every[None, None, :])
    safe = jnp.where(wave > 0, wave, jnp.float32(1.0))
    screen = -jnp.expm1(-wave / (4.0 * OMEGA * OMEGA)) / safe
    return jnp.where(wave > 0, screen, jnp.float32(1.0 / (4.0 * OMEGA * OMEGA)))


def hartley_rows(rows, points):
    product = rows[:, None] * jnp.arange(points, dtype=jnp.int32)[None, :] % points
    angle = product.astype(jnp.float32) * (2.0 * math.pi / points)
    return jnp.cos(angle) + jnp.sin(angle)


def mult(form, left, right):
    return jnp.einsum(form, left, right, precision=lax.Precision.HIGH)


def ring_place(band, bands):
    half = lax.div(band, 2)
    odd = lax.rem(band, 2)
    return (1 - odd) * half + odd * (bands - 1 - half)


def gather_kernel(
    bands,
    plan,
    section,
    cross_out,
    side_out,
    side_cross_out,
    stream_out,
    side_stream_out,
    cross,
    landed,
    stream,
    cross_send,
    cross_recv,
    ring_send,
    ring_recv,
    side_send,
    side_recv,
    keep,
):
    chunks, width = cross.shape[0], cross.shape[-1]
    half = chunks // 2
    steps = landed.shape[1]
    band, here = lax.axis_index("band"), lax.axis_index("grid")
    place = ring_place(band, bands)

    def member(spot):
        back = lax.div(spot, bands // 2)
        return (1 - back) * 2 * spot + back * (2 * (bands - 1 - spot) + 1)

    ring = (
        {"band": member(lax.rem(place + 1, bands))},
        {"band": member(lax.rem(place + bands - 1, bands))},
    )
    partner = {"grid": lax.rem(here + 2, 4)}
    sibling = {"grid": here + 1 - 2 * lax.rem(here, 2)}

    barrier = pltpu.get_barrier_semaphore()
    for other in (*ring, partner, sibling):
        pl.semaphore_signal(barrier, inc=1, device_id=other, device_id_type=MESH)
    pl.semaphore_wait(barrier, 4)

    def remote(source, target, send, recv, device):
        return pltpu.make_async_remote_copy(
            src_ref=source,
            dst_ref=target,
            send_sem=send,
            recv_sem=recv,
            device_id=device,
            device_id_type=MESH,
        )

    def lanes(k):
        return pl.ds(pl.multiple_of(k * width, 128), width)

    def cross_copy(k):
        return remote(
            section.at[:, :, :, lanes(k)], cross.at[k], cross_send.at[k], cross_recv.at[k], partner
        )

    lines = [(way, (part, j)) for part in range(2) for j in range(2) for way in range(2)]

    def ring_copy(way, part, t):
        return remote(
            stream.at[way, t, *part],
            landed.at[way, t, *part],
            ring_send.at[way, *part, t],
            ring_recv.at[way, *part, t],
            ring[way],
        )

    bounds = ((0, half), (half, half), (chunks, steps + 1 - chunks))

    def side_copy(k):
        if k == 0:
            source, target = section, side_out
        elif k == 1:
            source, target = cross, side_cross_out
        else:
            cut = pl.ds(*bounds[k - 2])
            source, target = stream.at[:, cut], side_stream_out.at[:, cut]
        return remote(source, target, side_send.at[k], side_recv.at[k], sibling)

    def keep_copy(k):
        if k == 0:
            return pltpu.make_async_copy(cross, cross_out, keep.at[k])
        cut = pl.ds(*bounds[k - 1])
        return pltpu.make_async_copy(stream.at[:, cut], stream_out.at[:, cut], keep.at[k])

    def store(part):
        side_copy(part + 2).start()
        keep_copy(part + 1).start()

    root = plan[lax.div(here, 2)]
    mine = jnp.full(stream.shape[4:], root, jnp.int32) == band

    @pl.loop(0, half)
    def _(k):
        cross_copy(k).start()
        cross_copy(half + k).start()

    for way, part in lines:
        stream[way, 0, *part] = section[*part, :, way * half * width : (way * half + 1) * width]
        ring_copy(way, part, 0).start()
    side_copy(0).start()

    @pl.loop(1, half)
    def _(t):
        for way, part in lines:
            ring_copy(way, part, t - 1).wait_recv()
            own = section[*part, :, lanes(way * half + t)]
            stream[way, t, *part] = jnp.where(mine, own, landed[way, t - 1, *part])
            ring_copy(way, part, t).start()

    store(0)

    @pl.loop(half, chunks)
    def _(t):
        for way in range(2):
            cross_copy(way * half + t - half).wait_recv()
        for way, part in lines:
            ring_copy(way, part, t - 1).wait_recv()
            own = cross[way * half + t - half, *part]
            stream[way, t, *part] = jnp.where(mine, own, landed[way, t - 1, *part])
            ring_copy(way, part, t).start()

    store(1)
    side_copy(1).start()
    keep_copy(0).start()

    @pl.loop(chunks, steps)
    def _(t):
        for way, part in lines:
            ring_copy(way, part, t - 1).wait_recv()
            stream[way, t, *part] = landed[way, t - 1, *part]
            ring_copy(way, part, t).start()

    for way, part in lines:
        ring_copy(way, part, steps - 1).wait_recv()
        stream[way, steps, *part] = landed[way, steps - 1, *part]
    store(2)

    @pl.loop(0, chunks)
    def _(k):
        cross_copy(k).wait_send()

    @pl.loop(0, steps)
    def _(t):
        for way, part in lines:
            ring_copy(way, part, t).wait_send()

    for k in range(5):
        side_copy(k).wait()
    for k in range(4):
        keep_copy(k).wait()


def gather(section, plan, bands, width):
    height, plane = section.shape[2], section.shape[3]
    chunks = plane // width
    steps = chunks + bands - 2
    piece = (2, 2, height, width)
    whole = jax.ShapeDtypeStruct((chunks, *piece), jnp.float32)
    log = jax.ShapeDtypeStruct((2, steps + 1, *piece), jnp.float32)
    dma = pltpu.SemaphoreType.DMA
    return pl.pallas_call(
        functools.partial(gather_kernel, bands),
        out_shape=(whole, jax.ShapeDtypeStruct(section.shape, jnp.float32), whole, log, log),
        in_specs=[
            pl.BlockSpec(memory_space=pltpu.SMEM),
            pl.BlockSpec(memory_space=pltpu.VMEM),
        ],
        out_specs=[pl.BlockSpec(memory_space=pl.ANY)] * 5,
        scratch_shapes=[
            pltpu.VMEM(whole.shape, jnp.float32),
            pltpu.VMEM((2, steps, *piece), jnp.float32),
            pltpu.VMEM(log.shape, jnp.float32),
            dma((chunks,)),
            dma((chunks,)),
            dma((2, 2, 2, steps)),
            dma((2, 2, 2, steps)),
            dma((5,)),
            dma((5,)),
            dma((4,)),
        ],
        compiler_params=pltpu.CompilerParams(
            collective_id=0, has_side_effects=True, vmem_limit_bytes=VMEM_BYTES
        ),
    )(plan, section)


def halves(value):
    high = value.astype(jnp.bfloat16)
    return high, (value - high.astype(jnp.float32)).astype(jnp.bfloat16)


def dot(left, right, axis=0):
    return lax.dot_general(
        left, right, (((1,), (axis,)), ((), ())), preferred_element_type=jnp.float32
    )


def three(left, right, axis=0):
    return dot(left[0], right[0], axis) + (dot(left[0], right[1], axis) + dot(left[1], right[0], axis))


def concat(pieces):
    return jnp.concatenate(pieces, axis=0)


def forward_kernel(
    points,
    info,
    square_z,
    decay_z,
    s0,
    s1,
    s2,
    s3,
    o0,
    o1,
    o2,
    o3,
    zcut_high,
    zcut_low,
    x_high,
    x_low,
    y_pair,
    y_low,
    square_xy,
    decay_xy,
    work,
):
    step = pl.program_id(0)
    width = x_high.shape[0]
    tiles = work.shape[0]
    window = zcut_high.shape[2]
    rows = pl.ds(pl.multiple_of(step * width, width), width)

    def source(part, j):
        return concat([s[0, 0, part, j] for s in (s0, s1, s2, s3)])

    own_re, own_im = (
        jnp.concatenate([o0[p, 0], o1[p, 0], o2[0, p, 0], o3[0, p, 0]], axis=0)
        for p in range(2)
    )
    fields = []
    for j in range(2):
        s_re, s_im = source(0, j), source(1, j)
        fields.append(s_re * own_re + s_im * own_im)
        fields.append(s_re * own_im - s_im * own_re)
    high, low = halves(jnp.concatenate(fields, axis=0))
    parts = []
    for k in range(2):
        cut = slice(k * (width - window), k * (width - window) + window)
        parts.append(
            three((zcut_high[k], zcut_low[k]), (high[:, cut], low[:, cut]), 1)
        )
    along = halves(jnp.concatenate(parts, axis=0))
    out = three(along, (x_high[...], x_low[...]))
    for k in range(tiles):
        work[k, rows, :] = out[:, 128 * k : 128 * (k + 1)]

    @pl.when(step == pl.num_programs(0) - 1)
    def _():
        scale = 1.0 / (points * points * points)

        def across(value):
            high, low = halves(value)
            return dot(y_pair[...], jnp.concatenate([high, low], axis=0)) + dot(y_low[...], high)

        @pl.loop(0, points // 4)
        def _(group):
            for pair in range(2):
                first = group * 4 + pair * 2
                lines = [pl.ds(first + u, points, stride=points) for u in range(2)]
                value = jnp.concatenate(
                    [work[k, line, :] for line in lines for k in range(tiles)], axis=1
                )
                factors = []
                for u in range(2):
                    wave = square_xy[...] + square_z[first + u]
                    safe = jnp.where(wave > 0, wave, 1.0)
                    screen = (scale - decay_xy[...] * (decay_z[first + u] * scale)) / safe
                    factors.append(
                        jnp.where(wave > 0, screen, scale / (4.0 * OMEGA * OMEGA))
                    )
                value = across(across(value) * jnp.concatenate(factors, axis=1))
                for u in range(2):
                    for k in range(tiles):
                        at = 128 * (u * tiles + k)
                        work[k, lines[u], :] = value[:, at : at + 128]

def inverse_kernel(info, weight, work, s0, s1, x_high, x_low, z_high, z_low, term):
    middle = term.shape[1]
    spectrum = halves(jnp.concatenate([work[k] for k in range(work.shape[0])], axis=1))
    along = halves(three((x_high[...], x_low[...]), spectrum, 1))
    field = three(along, (z_high[...], z_low[...]))
    term_re = term_im = 0.0
    for j in range(2):
        v_re = field[2 * j * middle : (2 * j + 1) * middle]
        v_im = field[(2 * j + 1) * middle : (2 * j + 2) * middle]
        s_re, s_im = (concat([s[0, 0, part, j] for s in (s0, s1)]) for part in range(2))
        term_re = term_re + weight[j] * (s_re * v_re - s_im * v_im)
        term_im = term_im + weight[j] * (s_re * v_im + s_im * v_re)
    term[0] = term_re
    term[1] = term_im


def numpy_hartley(points):
    index = np.arange(points)
    angle = index[:, None] * index[None, :] % points * (2.0 * math.pi / points)
    return np.cos(angle) + np.sin(angle)


def numpy_split(value):
    high = value.astype(ml_dtypes.bfloat16)
    return high, (value - high.astype(np.float64)).astype(ml_dtypes.bfloat16)


def solve(section, gathered, plan, weights, bands, width):
    cross, side, side_cross, stream, side_stream = gathered
    height, plane = section.shape[2], section.shape[3]
    points = 4 * height
    chunks = plane // width
    half = chunks // 2
    middle = points // 2
    here = lax.axis_index("grid")
    place = ring_place(lax.axis_index("band"), bands)
    root = ring_place(jnp.where(here // 2 == 0, plan[0], plan[1]), bands)
    info = jnp.stack(
        [lax.rem(place - root + bands, bands), lax.rem(root - place + bands, bands), here % 2]
    ).astype(jnp.int32)

    along = numpy_hartley(points)
    orders = [
        np.concatenate([(g ^ k) * height + np.arange(height) for k in range(4)]) for g in range(4)
    ]
    x_all = np.stack([np.kron(np.eye(4), along[order]) for order in orders])
    x_sides = x_all.reshape(4, 4, 2, middle, width)

    def pick(table):
        return [
            lax.dynamic_index_in_dim(jnp.asarray(piece), here, 0, keepdims=False)
            for piece in numpy_split(table)
        ]

    x_high, x_low = pick(x_all)
    z_high, z_low = numpy_split(np.kron(np.eye(4), along))
    y_high, y_low = numpy_split(along)
    window = -(-(width // 2) // 128) * 128

    def cuts(matrix):
        return jnp.asarray(
            np.stack([matrix[: width // 2, :window], matrix[width // 2 :, width - window :]])
        )

    index = np.arange(points)
    fold = np.where(index <= points // 2, index, index - points)
    square = (2.0 * math.pi / BOX) ** 2 * (fold * fold)
    decay = np.exp(-square / (4.0 * OMEGA * OMEGA))

    def single(value):
        return jnp.asarray(value.astype(np.float32))

    tables = [
        cuts(z_high),
        cuts(z_low),
        x_high,
        x_low,
        jnp.asarray(np.concatenate([y_high, y_high], axis=1)),
        jnp.asarray(y_low),
        single(square[:, None] + np.tile(square, 4)[None, :]),
        single(decay[:, None] * np.tile(decay, 4)[None, :]),
    ]

    def line(offset, first=0):
        def spot(i, info):
            way = lax.div(first + i, half)
            return (way, info[way] + lax.rem(i, half) + offset, 0, 0, 0, 0)

        return pl.BlockSpec((1, 1, 2, 2, height, width), spot)

    natural = pl.BlockSpec((2, 1, height, width), lambda i, info: (0, info[2], 0, i))
    piece = pl.BlockSpec((1, 2, 1, height, width), lambda i, info: (i, 0, info[2], 0, 0))
    scalars = pl.BlockSpec(memory_space=pltpu.SMEM)
    tiles = width // 128

    def full(table):
        return pl.BlockSpec(table.shape, lambda i, info: (0,) * table.ndim)

    spectrum = jax.ShapeDtypeStruct((tiles, plane, 128), jnp.float32)
    params = pltpu.CompilerParams(
        dimension_semantics=("arbitrary",), vmem_limit_bytes=VMEM_BYTES
    )
    work = pl.pallas_call(
        functools.partial(forward_kernel, points),
        grid_spec=pltpu.PrefetchScalarGridSpec(
            num_scalar_prefetch=1,
            grid=(chunks,),
            in_specs=[scalars] * 2
            + [line(0), line(0), line(half), line(half)]
            + [natural, natural, piece, piece]
            + [full(table) for table in tables],
            out_specs=full(spectrum),
        ),
        out_shape=spectrum,
        compiler_params=params,
    )(
        info,
        single(square),
        single(decay),
        stream,
        side_stream,
        stream,
        side_stream,
        section,
        side,
        cross,
        side_cross,
        *tables,
    )

    def inverse(part, side):
        first = side * half
        constants = [
            *pick(x_sides[:, :, part].reshape(4, 4 * middle, width)),
            jnp.asarray(z_high),
            jnp.asarray(z_low),
        ]
        return pl.pallas_call(
            inverse_kernel,
            grid_spec=pltpu.PrefetchScalarGridSpec(
                num_scalar_prefetch=1,
                grid=(half,),
                in_specs=[
                    scalars,
                    pl.BlockSpec((tiles, width, 128), lambda i, info: (0, first + i, 0)),
                ]
                + [line(part * half, first)] * 2
                + [full(table) for table in constants],
                out_specs=pl.BlockSpec((2, middle, width), lambda i, info: (0, 0, i)),
            ),
            out_shape=jax.ShapeDtypeStruct((2, middle, half * width), jnp.float32),
            compiler_params=params,
            cost_estimate=pl.CostEstimate(
                flops=12 * middle * width * plane, bytes_accessed=16 * plane * width, transcendentals=0
            ),
        )(info, weights, work, stream, side_stream, *constants)

    return inverse


def per_device(orbitals, local_potential, plan, occupancy):
    rounds = plan.shape[0]
    count_own = orbitals.shape[1]
    height = orbitals.shape[2]
    plane = orbitals.shape[3]
    points = math.isqrt(plane)
    devices = lax.axis_size("grid")
    parts = devices // 4
    here = lax.axis_index("grid")
    share, slot = here // parts, here % parts
    first_core, first_chip = share % 2 == 0, share // 2 == 0
    teams = [[q * parts + s for s in range(parts)] for q in range(4)]

    def swap(value, bit):
        return lax.ppermute(
            value, "grid", [(g, ((g // parts) ^ bit) * parts + g % parts) for g in range(devices)]
        )

    def core_swap(value):
        return swap(value, 1)

    def chip_swap(value):
        return swap(value, 2)

    def turn(value, split, concat):
        if parts == 1:
            return value
        return lax.all_to_all(
            value, "grid", split, concat, axis_index_groups=teams, tiled=True
        )

    k_first = jnp.stack([local_potential * orbitals[1], -local_potential * orbitals[0]])
    section = orbitals + TIME_STEP * k_first

    band = lax.axis_index("band")

    def spread(orbital):
        return lax.psum(
            jnp.stack([jnp.where(band == plan[r], orbital, 0.0) for r in range(rounds)]), "band"
        )

    def collect(both):
        near = jnp.where(first_chip, both[0], both[1])
        far = chip_swap(jnp.where(first_chip, both[1], both[0]))
        pair = jnp.stack([near, far])
        other = core_swap(pair)
        return jnp.concatenate([near, other[0], far, other[1]], axis=1)

    block = jnp.arange(parts)[:, None] + jnp.stack([(share ^ k) * parts for k in range(4)])
    order = block[:, :, None] * height + jnp.arange(height, dtype=jnp.int32)
    along_x = hartley_rows(order.reshape(points), points)
    ways = along_x.reshape(parts, 4, height, points)
    width = points // parts
    along = hartley_rows(jnp.arange(points, dtype=jnp.int32), points)
    source_group = jnp.where(first_chip, plan[0], plan[1])
    groups = jnp.arange(occupancy.shape[0], dtype=jnp.int32)
    filled = jnp.sum(jnp.where(groups == source_group, occupancy, 0))

    weights = [jnp.where(j < filled, 2.0, 0.0).astype(jnp.float32) for j in range(count_own)]
    bands = lax.axis_size("band")
    span = 4 * points
    if parts == 1 and span % 128 == 0 and height % 8 == 0 and count_own == rounds == 2 and bands > 2:
        scaled = -MIXING * jnp.stack(weights)
        gathered = gather(section, plan, bands, span)
        inverse = solve(section, gathered, plan, scaled, bands, span)
        far = [chip_swap(inverse(1, side)) for side in range(2)]
        near = [inverse(0, side) for side in range(2)]
    else:
        mine = jnp.where(first_core, section[:, 0], section[:, 1])
        give = jnp.where(first_core, section[:, 1], section[:, 0])
        half = jnp.concatenate([mine, core_swap(give)], axis=1)
        own = jnp.concatenate([half, chip_swap(half)], axis=1)

        kernel = screened_kernel(points, slot * width, width) * (1.0 / (points * points * points))
        def spectrum(source):
            dens_re = source[0] * own[0] + source[1] * own[1]
            dens_im = source[0] * own[1] - source[1] * own[0]
            field = jnp.stack([dens_re, dens_im]).reshape(2, 4 * height, points, points)
            field = mult("pxyz,zk->pxyk", field, along)
            field = turn(mult("pxyz,yk->pxkz", field, along), 2, 1)
            return mult("pxyz,xk->pkyz", field, along_x) * kernel

        def potential_term(source, weight, moved, side):
            rows = ways[:, 2 * side : 2 * side + 2].reshape(-1, points)
            field = turn(mult("pxyz,kx->pkyz", moved, rows), 1, 2)
            field = mult("pxyz,yk->pxkz", field, along)
            field = mult("pxyz,zk->pxyk", field, along)
            v_re, v_im = field.reshape(2, 2 * height, plane)
            s_re, s_im = source[:, 2 * side * height : 2 * (side + 1) * height]
            scale = -MIXING * weight
            return jnp.stack([scale * (s_re * v_re - s_im * v_im), scale * (s_re * v_im + s_im * v_re)])

        both = [spread(section[:, 0])]
        for j in range(1, count_own):
            both[j - 1], orbital = lax.optimization_barrier((both[j - 1], section[:, j]))
            both.append(spread(orbital))
        near = far = 0.0
        for j in range(count_own):
            if j > 0:
                both[j], near, far = lax.optimization_barrier((both[j], near, far))
            source = collect(both[j])
            moved = spectrum(source)
            far = far + potential_term(source, weights[j], moved, 1)
            if j == count_own - 1:
                far = chip_swap(far)
            near = near + potential_term(source, weights[j], moved, 0)
        near, far = [near], [far]
    got = [core_swap(a[:, height:] + b[:, height:]) for a, b in zip(near, far)]
    kept = [a[:, :height] + b[:, :height] for a, b in zip(near, far)]
    got, kept = jnp.concatenate(got, axis=2), jnp.concatenate(kept, axis=2)
    exchange = jnp.stack(
        [jnp.where(first_core, kept, got), jnp.where(first_core, got, kept)], axis=1
    )

    hamil = local_potential * section + exchange
    k_second = jnp.stack([hamil[1], -hamil[0]])
    delta = 0.5 * TIME_STEP * (k_first + k_second)
    inner = jnp.sum(orbitals * delta, axis=(0, 2, 3))
    squared_modulus = jnp.sum(delta * delta, axis=(0, 2, 3))
    energy = jnp.sum(section * hamil, axis=(0, 2, 3))
    inner, squared_modulus, energy = lax.psum(jnp.stack([inner, squared_modulus, energy]), "grid")
    factor = -2.0 * inner / (squared_modulus + 1e-06)
    fresh = orbitals + factor[None, :, None, None] * delta
    own_filled = jnp.sum(jnp.where(groups == band, occupancy, 0))
    filling = jnp.where(jnp.arange(count_own, dtype=jnp.int32) < own_filled, 2.0, 0.0).astype(
        jnp.float32
    )
    return (fresh, filling * energy / (points * points * points))


def solution(mesh):
    return jax.shard_map(
        per_device,
        mesh=mesh,
        in_specs=(P(None, "band", "grid", None), P("grid", None), P(), P()),
        out_specs=(P(None, "band", "grid", None), P("band")),
        check_vma=False,
    )
```
